32 devices in a mesh: group: 2 (over y), replica: 4 (over z), tensor: 4 (over x, core).
Axes of the slice: x: 2, y: 2, z: 4, core: 2. Of those that a mesh axis runs over, the one named last changes fastest.
Arguments:
- suffix_hidden: bfloat16 [2048, 8192], P(('group', 'replica'), 'tensor'), parts along dimension 0, may hold values from -6 to 6
- base_query: bfloat16 [2048, 8192], P(('group', 'replica'), 'tensor'), parts along dimension 0
- suffix_key_value: bfloat16 [2048, 8, 256], P(('group', 'replica'), 'tensor'), parts along dimension 0, may hold values from -6 to 6
- tenant_prefix_cache: bfloat16 [8, 1024, 8, 256], P(('group', 'replica'), None, 'tensor'), parts along dimension 0
- adapter_down: bfloat16 [2, 32, 8192], P(None, None, 'tensor'), may hold values from -0.0625 to 0.0625
- adapter_up_query: bfloat16 [2, 16, 8192], P(None, None, 'tensor'), may hold values from -1.5 to 1.5
- adapter_up_value: bfloat16 [2, 16, 8, 128], P(None, None, 'tensor'), may hold values from -1.5 to 1.5
- tenant_replica: int32 [8], P('group'), parts along dimension 0, may hold values from 0 to 3, as said below
- tenant_of_request: int32 [8], P(('group', 'replica')), parts along dimension 0, may hold values from 0 to 3, as said below
- suffix_blocks: int32 [8], P(('group', 'replica')), parts along dimension 0, may hold values from 1 to 2, as said below
- request_adapter: int32 [8], P(('group', 'replica')), parts along dimension 0, may hold values from 0 to 1
Outputs:
- attended: bfloat16 [2048, 8192], P(('group', 'replica'), 'tensor'), parts along dimension 0
The draws below stay inside these ranges and needn't reach their ends.
There are 2 independent parts, one for each index of `group`. The reference program is written for one: setup_inputs(seed, part) draws one part's arguments, and reference() takes and returns one part's arrays. A program takes and returns all parts, laid end to end along the dimension named above; an argument that names none is the same for every part. Nothing has to cross between parts.
Inputs may be any that keep to these rules, and one draw needn't show every extreme that they name: `tenant_replica`: each replica owns exactly one tenant. `tenant_of_request`: the owner of a replica's tenant lies 0 to 3 replicas before it in cycle order (owner = index minus distance, modulo 4); some replica reads at distance 4 - 1. `suffix_blocks`: some replica's request has 2 blocks.
All inputs are finite; a program needn't handle non-finite values.
Results may differ from the reference program's by a relative error of at most 0.012.
Values may be sent and summed in bfloat16 or wider, within the bound.
No kernel may reach another device: no remote copies, remote signals or barrier semaphores. Data moves between devices by JAX's collectives and lax.ppermute only.
A program may use at most 64 MiB of HBM per device.

```python
import math
import jax
import jax.numpy as jnp
from jax import lax

MODEL_WIDTH = 8192
QUERY_HEADS = 64
KEY_HEADS = 8
HEAD_SIZE = 128
ADAPTER_RANK = 16
ADAPTER_COUNT = 2
PREFIX = 1024
STRETCH = 128
STRETCHES = 2
READ_SPAN = 4
ROWS = 256
TENANTS = 4
TOKENS = 1024


def shared_routes(key):
    owner = jax.random.permutation(jax.random.fold_in(key, 11), TENANTS).astype(jnp.int32)
    distance = jax.random.randint(jax.random.fold_in(key, 12), (TENANTS,), 0, READ_SPAN)
    farthest = jax.random.randint(jax.random.fold_in(key, 13), (), 0, TENANTS)
    distance = jnp.where(jnp.arange(TENANTS) == farthest, READ_SPAN - 1, distance)
    source = jnp.remainder(jnp.arange(TENANTS) - distance, TENANTS)
    inverse = jnp.argsort(owner, stable=True)
    tenant = inverse[source].astype(jnp.int32)
    return (owner, tenant)


def draw_tenant_replica(key, part):
    owner, tenant = shared_routes(key)
    return owner


def draw_tenant_of_request(key, part):
    owner, tenant = shared_routes(key)
    return tenant


def draw_suffix_blocks(key, part):
    key = jax.random.fold_in(key, 7)
    raw = jax.random.randint(jax.random.fold_in(key, 1), (TENANTS,), 0, STRETCHES)
    blocks = 1 + jnp.remainder(raw + part, STRETCHES)
    fullest = jax.random.randint(jax.random.fold_in(key, 2), (), 0, TENANTS)
    blocks = jnp.where(jnp.arange(TENANTS) == fullest, STRETCHES, blocks)
    return blocks.astype(jnp.int32)


def draw_base_query(key, part):
    key = jax.random.fold_in(key, 3)
    values = jax.random.normal(jax.random.fold_in(key, 1), (TOKENS, QUERY_HEADS * HEAD_SIZE), jnp.float32)
    return values.astype(jnp.bfloat16)


def draw_tenant_prefix_cache(key, part):
    key = jax.random.fold_in(key, 5)
    values = jax.random.normal(jax.random.fold_in(key, 1), (TENANTS, PREFIX, KEY_HEADS, 2 * HEAD_SIZE), jnp.float32)
    return values.astype(jnp.bfloat16)


def plant(values, rng, least, high):
    place = [jax.random.randint(jax.random.fold_in(rng, axis), (), 0, length) for axis, length in enumerate(values.shape)]
    longest = values.shape.index(max(values.shape))
    beside = place[:longest] + [(place[longest] + 1) % values.shape[longest]] + place[longest + 1:]
    return values.at[tuple(place)].set(least).at[tuple(beside)].set(high)


def block_levels(stream_key, extent, shards, least, high):
    gain, own = 1.0, jax.random.fold_in(stream_key, 6)
    for dim, blocks in shards:
        heights = jnp.exp(jax.random.uniform(jax.random.fold_in(own, dim), (blocks,), jnp.float32, least / len(shards), high / len(shards)))
        gain = gain * jnp.repeat(heights, extent[dim] // blocks).reshape([-1 if axis == dim else 1 for axis in range(len(extent))])
    return gain


def scatter_about(stream_key, shape, scale, limit, split=(), dtype=jnp.bfloat16):
    drawn = scale * jax.random.normal(stream_key, shape, jnp.float32)
    if split:
        drawn = drawn * block_levels(stream_key, shape, split, -0.22, 0.18)
    return jnp.clip(drawn, -limit, limit).astype(dtype)


def setup_inputs(seed: int = 0, part: int = 0) -> dict:
    key_list = jax.random.split(jax.random.key(seed), 12)
    part_keys = jax.random.split(jax.random.fold_in(key_list[11], part), 12)
    suffix_hidden = scatter_about(part_keys[0], (TOKENS, MODEL_WIDTH), 1.0, 6.0, ((0, 4), (1, 4)))
    base_query = draw_base_query(jax.random.fold_in(jax.random.fold_in(key_list[11], part), 71), part)
    suffix_key_value = scatter_about(part_keys[2], (TOKENS, KEY_HEADS, 2 * HEAD_SIZE), 1.0, 6.0, ((0, 4), (1, 4)))
    tenant_prefix_cache = draw_tenant_prefix_cache(jax.random.fold_in(jax.random.fold_in(key_list[11], part), 71), part)
    adapter_down = scatter_about(key_list[4], (ADAPTER_COUNT, 2 * ADAPTER_RANK, MODEL_WIDTH), MODEL_WIDTH ** -0.5, 0.0625, ((2, 4),))
    adapter_up_query = scatter_about(key_list[5], (ADAPTER_COUNT, ADAPTER_RANK, QUERY_HEADS * HEAD_SIZE), ADAPTER_RANK ** -0.5, 1.5, ((2, 4),))
    adapter_up_value = scatter_about(key_list[6], (ADAPTER_COUNT, ADAPTER_RANK, KEY_HEADS, HEAD_SIZE), ADAPTER_RANK ** -0.5, 1.5, ((2, 4),))
    tenant_replica = draw_tenant_replica(jax.random.fold_in(jax.random.fold_in(key_list[11], part), 71), part)
    tenant_of_request = draw_tenant_of_request(jax.random.fold_in(jax.random.fold_in(key_list[11], part), 71), part)
    suffix_blocks = draw_suffix_blocks(jax.random.fold_in(jax.random.fold_in(key_list[11], part), 71), part)
    request_adapter = plant(jax.random.randint(part_keys[10], (TENANTS,), 0, ADAPTER_COUNT), jax.random.fold_in(part_keys[10], 1), 0, ADAPTER_COUNT - 1).astype(jnp.int32)
    return dict(suffix_hidden=suffix_hidden, base_query=base_query, suffix_key_value=suffix_key_value, tenant_prefix_cache=tenant_prefix_cache, adapter_down=adapter_down, adapter_up_query=adapter_up_query, adapter_up_value=adapter_up_value, tenant_replica=tenant_replica, tenant_of_request=tenant_of_request, suffix_blocks=suffix_blocks, request_adapter=request_adapter)


def attend(query, all_keys, values, prefix_len):
    row_count = query.shape[0]
    scores = jnp.einsum('rgd,kd->grk', query.astype(jnp.float32), all_keys.astype(jnp.float32)) / math.sqrt(HEAD_SIZE)
    key_index = jnp.arange(all_keys.shape[0])
    row_index = jnp.arange(row_count)
    allowed = (key_index[None, :] < prefix_len) | (key_index[None, :] - prefix_len <= row_index[:, None])
    scores = jnp.where(allowed[None], scores, -jnp.inf)
    largest = lax.optimization_barrier(jnp.max(scores, axis=2, keepdims=True))
    powers = jnp.exp(scores - largest)
    weights = (powers / lax.optimization_barrier(jnp.sum(powers, axis=2, keepdims=True))).astype(jnp.bfloat16)
    return jnp.einsum('grk,kd->rgd', weights.astype(jnp.float32), values.astype(jnp.float32)).astype(jnp.bfloat16)

def request_attention(row_input, query_input, suffix_input, prefix_block, suffix_block_count, adapter_choice, adapter_down, adapter_up_query, adapter_up_value):
    down_matrix_rows = adapter_down[adapter_choice]
    rank_projection = jnp.dot(row_input, down_matrix_rows.T, preferred_element_type=jnp.float32).astype(jnp.bfloat16)
    query_update = jnp.dot(rank_projection[:, :ADAPTER_RANK], adapter_up_query[adapter_choice], preferred_element_type=jnp.float32)
    query = (query_input.astype(jnp.float32) + query_update).astype(jnp.bfloat16)
    value_up_matrix = adapter_up_value[adapter_choice].reshape(ADAPTER_RANK, KEY_HEADS * HEAD_SIZE)
    value_delta = jnp.dot(rank_projection[:, ADAPTER_RANK:], value_up_matrix, preferred_element_type=jnp.float32).reshape(ROWS, KEY_HEADS, HEAD_SIZE)
    suffix_value = (suffix_input[..., HEAD_SIZE:].astype(jnp.float32) + value_delta).astype(jnp.bfloat16)
    all_keys = jnp.concatenate([prefix_block[..., :HEAD_SIZE], suffix_input[..., :HEAD_SIZE]], axis=0)
    values = jnp.concatenate([prefix_block[..., HEAD_SIZE:], suffix_value], axis=0)
    grouped = query.reshape(ROWS, KEY_HEADS, QUERY_HEADS // KEY_HEADS, HEAD_SIZE)
    per_head = [attend(grouped[:, head], all_keys[:, head], values[:, head], PREFIX) for head in range(KEY_HEADS)]
    result = jnp.stack(per_head, axis=1).reshape(ROWS, QUERY_HEADS * HEAD_SIZE)
    live_rows = jnp.arange(ROWS) < suffix_block_count * STRETCH
    return jnp.where(live_rows[:, None], result, jnp.zeros_like(result))

def reference(suffix_hidden, base_query, suffix_key_value, tenant_prefix_cache, adapter_down, adapter_up_query, adapter_up_value, tenant_replica, tenant_of_request, suffix_blocks, request_adapter):
    rows_all = suffix_hidden.reshape(TENANTS, ROWS, MODEL_WIDTH)
    query_all = base_query.reshape(TENANTS, ROWS, QUERY_HEADS * HEAD_SIZE)
    suffix_all = suffix_key_value.reshape(TENANTS, ROWS, KEY_HEADS, 2 * HEAD_SIZE)
    owner_slot = tenant_replica[tenant_of_request].astype(jnp.int32)

    def one_replica(items):
        row_input, query_input, suffix_input, slot, suffix_block_count, adapter_choice = items
        prefix_block = lax.dynamic_index_in_dim(tenant_prefix_cache, slot, 0, keepdims=False)
        return request_attention(row_input, query_input, suffix_input, prefix_block, suffix_block_count, adapter_choice, adapter_down, adapter_up_query, adapter_up_value)
    result = lax.map(one_replica, (rows_all, query_all, suffix_all, owner_slot, suffix_blocks, request_adapter))
    return result.reshape(TOKENS, QUERY_HEADS * HEAD_SIZE)
```

```python
import functools
import math

import jax
import jax.numpy as jnp
from jax import lax
from jax.experimental import pallas as pl
from jax.experimental.pallas import tpu as pltpu
from jax.sharding import PartitionSpec as P

STRETCH = 128
READ_SPAN = 4
CHUNKS = 4
VMEM_BYTES = 40 * 1024 * 1024
NT = (((1,), (1,)), ((), ()))
TN = (((0,), (0,)), ((), ()))


def swap_sum(value, axis):
    size = lax.axis_size(axis)
    if size & (size - 1):
        return lax.psum(value, axis)
    step = 1
    while step < size:
        value = value + lax.ppermute(value, axis, [(i, i ^ step) for i in range(size)])
        step *= 2
    return value


def head_scores(query, keys):
    return lax.dot_general(query, keys, NT, preferred_element_type=jnp.float32)


def with_ones(values):
    return jnp.concatenate([values, jnp.ones_like(values)], axis=1)


def wide(column, count):
    return jnp.concatenate([column] * count, axis=1) if count > 1 else column


def prepare_kernel(
    heads, group, width, rank, scale,
    choice_ref, low_ref, base_ref, up_query_ref, up_value_ref, suffix_ref,
    query_ref, largest_ref, total_ref, weighted_ref,
):
    rows = base_ref.shape[0]
    choice = choice_ref[0]
    low = low_ref[...].astype(jnp.bfloat16)
    update = lax.dot_general(low[:rank], up_query_ref[choice], TN, preferred_element_type=jnp.float32)
    query_ref[...] = (base_ref[...].astype(jnp.float32) + update).astype(jnp.bfloat16)
    delta = lax.dot_general(low[rank:], up_value_ref[choice], TN, preferred_element_type=jnp.float32)
    row = lax.broadcasted_iota(jnp.int32, (rows, rows), 0)
    column = lax.broadcasted_iota(jnp.int32, (rows, rows), 1)
    seen = column <= row
    for head in range(heads):
        start = 2 * width * head
        keys = suffix_ref[:, start : start + width]
        base_value = suffix_ref[:, start + width : start + 2 * width].astype(jnp.float32)
        values = (base_value + delta[:, head * width : (head + 1) * width]).astype(jnp.bfloat16)
        both = with_ones(values)
        for member in range(group):
            at = slice((head * group + member) * width, (head * group + member + 1) * width)
            scores = jnp.where(seen, head_scores(query_ref[:, at], keys), -jnp.inf)
            largest = jnp.broadcast_to(jnp.max(scores, axis=1, keepdims=True), (rows, width))
            powers = jnp.exp2((scores - wide(largest, rows // width)) * scale)
            summed = jnp.dot(powers.astype(jnp.bfloat16), both, preferred_element_type=jnp.float32)
            largest_ref[:, at] = largest
            weighted_ref[:, at] = summed[:, :width]
            total_ref[:, at] = summed[:, width:]


def chunk_kernel(heads, group, width, scale, last, *refs):
    if last:
        blocks_ref, query_ref, page_ref, largest_ref, total_ref, weighted_ref, out_ref = refs
    else:
        query_ref, page_ref, largest_ref, total_ref, weighted_ref, largest_out, total_out, weighted_out = refs
    rows, count = query_ref.shape[0], page_ref.shape[0]
    if last:
        live = lax.broadcasted_iota(jnp.int32, (rows, width), 0) < blocks_ref[0] * STRETCH
    for head in range(heads):
        start = 2 * width * head
        keys = page_ref[:, start : start + width]
        both = with_ones(page_ref[:, start + width : start + 2 * width])
        for member in range(group):
            at = slice((head * group + member) * width, (head * group + member + 1) * width)
            scores = head_scores(query_ref[:, at], keys)
            before = largest_ref[:, at]
            largest = jnp.maximum(before, jnp.max(scores, axis=1, keepdims=True))
            powers = jnp.exp2((scores - wide(largest, count // width)) * scale)
            summed = jnp.dot(powers.astype(jnp.bfloat16), both, preferred_element_type=jnp.float32)
            fade = jnp.exp2((before - largest) * scale)
            weighted = weighted_ref[:, at] * fade + summed[:, :width]
            total = total_ref[:, at] * fade + summed[:, width:]
            if last:
                result = jnp.where(live, weighted / total, 0.0)
                out_ref[:, at] = result.astype(jnp.bfloat16)
            else:
                largest_out[:, at] = largest
                weighted_out[:, at] = weighted
                total_out[:, at] = total


def in_vmem(array):
    return pltpu.with_memory_space_constraint(array, pltpu.VMEM)


def cost(rows, columns, keys):
    return pl.CostEstimate(
        flops=4 * rows * columns * keys, bytes_accessed=4 * rows * columns, transcendentals=0
    )


WHOLE = pl.BlockSpec(memory_space=pltpu.VMEM)
SCALARS = pl.BlockSpec(memory_space=pltpu.SMEM)


def prepare(shape, choice, low, base_query, up_query, up_value, suffix):
    heads, group, width, rank, scale = shape
    rows, columns = base_query.shape
    state = pltpu.VMEM((rows, columns), jnp.float32)
    return pl.pallas_call(
        functools.partial(prepare_kernel, heads, group, width, rank, scale),
        out_shape=(pltpu.VMEM((rows, columns), jnp.bfloat16), state, state, state),
        in_specs=[SCALARS] + [WHOLE] * 5,
        out_specs=(WHOLE,) * 4,
        compiler_params=pltpu.CompilerParams(vmem_limit_bytes=VMEM_BYTES),
        cost_estimate=cost(rows, columns, rows),
        name="prepare",
    )(choice, low, base_query, up_query, up_value, suffix)


def add_chunk(shape, query, page, state):
    heads, group, width, rank, scale = shape
    rows, columns = query.shape
    one = pltpu.VMEM((rows, columns), jnp.float32)
    return pl.pallas_call(
        functools.partial(chunk_kernel, heads, group, width, scale, False),
        out_shape=(one,) * 3,
        in_specs=[WHOLE] * 5,
        out_specs=(WHOLE,) * 3,
        input_output_aliases={2: 0, 3: 1, 4: 2},
        compiler_params=pltpu.CompilerParams(vmem_limit_bytes=VMEM_BYTES),
        cost_estimate=cost(rows, columns, page.shape[0]),
        name="add_chunk",
    )(in_vmem(query), in_vmem(page), *map(in_vmem, state))


def finish(shape, blocks, query, page, state):
    heads, group, width, rank, scale = shape
    rows, columns = query.shape
    return pl.pallas_call(
        functools.partial(chunk_kernel, heads, group, width, scale, True),
        out_shape=jax.ShapeDtypeStruct((rows, columns), jnp.bfloat16),
        in_specs=[SCALARS] + [WHOLE] * 5,
        out_specs=WHOLE,
        compiler_params=pltpu.CompilerParams(vmem_limit_bytes=VMEM_BYTES),
        cost_estimate=cost(rows, columns, page.shape[0]),
        name="finish",
    )(blocks, in_vmem(query), in_vmem(page), *map(in_vmem, state))


def tied(value, other):
    return lax.optimization_barrier((value, other))[0]


def line_attention(shape, page, owner, blocks, prepared):
    place = lax.axis_index("replica")
    depth = page.shape[0] // CHUNKS
    own = [page[k * depth : (k + 1) * depth].reshape(depth, -1) for k in range(CHUNKS)]

    outer_in, outer_out = [(0, 1), (3, 2)], [(1, 0), (2, 3)]
    edge, middle, far = {}, {}, {}
    edge[0] = lax.ppermute(own[0], "replica", outer_in)

    wanted = jnp.where(jnp.arange(4) == place, owner, 0)
    wanted = swap_sum(wanted, "replica")
    w0, w1, w2, w3 = (wanted[i] for i in range(4))
    cross_right = jnp.where(w2 <= 1, w2, w3)
    cross_left = jnp.where(w1 >= 2, w1, w0)
    at_left, at_right = place == 1, place == 2
    inside = at_left | at_right
    pass_on = (at_left & (cross_right == 0)) | (at_right & (cross_left == 3))
    send_own = (at_left & (w0 == 1)) | (at_right & (w3 == 2))
    far_passed = (at_left & (w3 == 0)) | (at_right & (w0 == 3))
    two_right = (w2 <= 1) & (w3 <= 1) & (w2 != w3)
    two_left = (w1 >= 2) & (w0 >= 2) & (w1 != w0)
    use_far = ((place == 3) & two_right) | ((place == 0) & two_left)
    second = (two_right | two_left).astype(jnp.int32).reshape(1)
    second = swap_sum(second, "group")[0] > 0
    read_own = owner == place
    read_outer = (at_left & (owner == 0)) | (at_right & (owner == 3))

    query, *state0 = prepared()

    for k in range(CHUNKS + 2):
        if k:
            if k < 2:
                edge[k] = lax.ppermute(own[k], "replica", outer_in)
            else:
                out = jnp.where(send_own, own[k - 2], middle[k - 2])
                if k < CHUNKS:
                    out = jnp.where(inside, out, own[k])
                    edge[k] = lax.ppermute(out, "replica", outer_in + outer_out)
                elif k < CHUNKS + 1:
                    edge[k] = lax.ppermute(out, "replica", outer_out)
                else:
                    last_out = out
        if k < CHUNKS:
            mine = own[k] if k < 2 else tied(own[k], middle[k - 2])
            middle[k] = lax.ppermute(
                jnp.where(pass_on, edge[k], mine), "replica", [(1, 2), (2, 1)]
            )

    def chosen(k, brought):
        across = jnp.where(read_outer, edge[k], middle[k]) if k < CHUNKS else middle[k]
        return jnp.where(read_own, own[k], jnp.where(inside, across, brought))

    first = [chosen(k, edge[k + 2]) for k in range(CHUNKS - 1)]

    def one_page():
        brought = lax.ppermute(last_out, "replica", outer_out)
        state = state0
        state = add_chunk(shape, query, jnp.concatenate(first, axis=0), state)
        return finish(shape, blocks, query, chosen(CHUNKS - 1, brought), state)

    def two_pages():
        for k in range(CHUNKS):
            far[k] = lax.ppermute(
                jnp.where(far_passed, edge[k], own[k]), "replica", [(1, 3), (2, 0)]
            )
        brought = lax.ppermute(last_out, "replica", outer_out)
        state = state0
        for k in range(CHUNKS - 1):
            state = add_chunk(shape, query, jnp.where(use_far, far[k], first[k]), state)
        k = CHUNKS - 1
        return finish(
            shape, blocks, query, chosen(k, jnp.where(use_far, far[k], brought)), state
        )

    return lax.cond(second, two_pages, one_page)


def ring_attention(shape, page, owner, blocks, prepared):
    size = lax.axis_size("replica")
    distance = jnp.remainder(lax.axis_index("replica") - owner, size)
    page = page.reshape(page.shape[0], -1)
    chosen = page
    for offset in range(1, READ_SPAN):
        moved = lax.ppermute(page, "replica", [(i, (i + offset) % size) for i in range(size)])
        chosen = jnp.where(distance == offset, moved, chosen)
    query, *state = prepared()
    half = page.shape[0] // 2
    state = add_chunk(shape, query, chosen[:half], state)
    return finish(shape, blocks, query, chosen[half:], state)


def on_device(
    suffix_hidden,
    base_query,
    suffix_key_value,
    tenant_prefix_cache,
    adapter_down,
    adapter_up_query,
    adapter_up_value,
    tenant_replica,
    tenant_of_request,
    suffix_blocks,
    request_adapter,
):
    rows = suffix_hidden.shape[0]
    heads, width = suffix_key_value.shape[1], suffix_key_value.shape[2] // 2
    group = base_query.shape[1] // (heads * width)
    adapters, rank = adapter_down.shape[0], adapter_down.shape[1] // 2
    shape = (heads, group, width, rank, math.log2(math.e) / math.sqrt(width))
    owner = tenant_replica[tenant_of_request[0]]

    def prepared():
        down = lax.dynamic_index_in_dim(adapter_down, request_adapter[0], 0, keepdims=False)
        low = lax.dot_general(down, suffix_hidden, NT, preferred_element_type=jnp.float32)
        low = swap_sum(low, "tensor")
        return prepare(
            shape,
            request_adapter,
            low,
            base_query,
            adapter_up_query,
            adapter_up_value.reshape(adapters, rank, heads * width),
            suffix_key_value.reshape(rows, heads * 2 * width),
        )

    attention = line_attention if lax.axis_size("replica") == 4 else ring_attention
    return attention(shape, tenant_prefix_cache[0], owner, suffix_blocks, prepared)


def solution(mesh):
    in_specs = (
        P(("group", "replica"), "tensor"),
        P(("group", "replica"), "tensor"),
        P(("group", "replica"), "tensor", None),
        P(("group", "replica"), None, "tensor", None),
        P(None, None, "tensor"),
        P(None, None, "tensor"),
        P(None, None, "tensor", None),
        P("group"),
        P(("group", "replica")),
        P(("group", "replica")),
        P(("group", "replica")),
    )
    out_specs = P(("group", "replica"), "tensor")
    return jax.shard_map(
        on_device, mesh=mesh, in_specs=in_specs, out_specs=out_specs, check_vma=False
    )
```

```python
import functools
import math

import jax
import jax.numpy as jnp
from jax import lax
from jax.experimental import pallas as pl
from jax.experimental.pallas import tpu as pltpu
from jax.sharding import PartitionSpec as P

STRETCH = 128
READ_SPAN = 4
VMEM_BYTES = 24 * 1024 * 1024
NT = (((1,), (1,)), ((), ()))
TN = (((0,), (0,)), ((), ()))


def swap_sum(value, axis):
    size = lax.axis_size(axis)
    if size & (size - 1):
        return lax.psum(value, axis)
    step = 1
    while step < size:
        value = value + lax.ppermute(value, axis, [(i, i ^ step) for i in range(size)])
        step *= 2
    return value


def head_scores(query, keys):
    return lax.dot_general(query, keys, NT, preferred_element_type=jnp.float32)


def with_ones(values):
    return jnp.concatenate([values, jnp.ones_like(values)], axis=1)


def wide(column, count):
    return jnp.concatenate([column] * count, axis=1) if count > 1 else column


def owner_of(places_ref, tenant_ref):
    return places_ref[tenant_ref[0]]


def copy_read(flags, page_ref, at, sources):
    for flag, source in zip(flags, sources):

        @pl.when(flag)
        def _():
            page_ref[at, :] = source[...]


def attend_part(shape, query_ref, at, keys, both, state, seen=None):
    heads, group, width, rank, scale = shape
    rows, depth = query_ref.shape[0], keys.shape[0]
    scores = head_scores(query_ref[:, at], keys)
    if seen is not None:
        scores = jnp.where(seen, scores, -jnp.inf)
    largest = jnp.broadcast_to(jnp.max(scores, axis=1, keepdims=True), (rows, width))
    if state is not None:
        before, weighted_before, total_before = state
        largest = jnp.maximum(before, largest)
        fade = jnp.exp2((before - largest) * scale)
    powers = jnp.exp2((scores - wide(largest, depth // width)) * scale)
    summed = jnp.dot(powers.astype(jnp.bfloat16), both, preferred_element_type=jnp.float32)
    weighted, total = summed[:, :width], summed[:, width:]
    if state is not None:
        weighted, total = weighted + weighted_before * fade, total + total_before * fade
    return largest, weighted, total


def first_kernel(shape, read_flags, cuts, routes, *refs):
    heads, group, width, rank, scale = shape
    places_ref, tenant_ref, choice_ref, low_ref, base_ref, up_query_ref, up_value_ref, suffix_ref = refs[:8]
    sources, (query_ref, largest_ref, weighted_ref, total_ref, page_ref) = refs[8:-5], refs[-5:]
    rows = base_ref.shape[0]
    choice = choice_ref[0]
    low = low_ref[...].astype(jnp.bfloat16)
    update = lax.dot_general(low[:rank], up_query_ref[choice], TN, preferred_element_type=jnp.float32)
    query_ref[...] = (base_ref[...].astype(jnp.float32) + update).astype(jnp.bfloat16)
    delta = lax.dot_general(low[rank:], up_value_ref[choice], TN, preferred_element_type=jnp.float32)
    flags = read_flags(owner_of(places_ref, tenant_ref))
    for part, (begin, end) in enumerate(cuts):
        copy_read(flags, page_ref, slice(begin, end), sources[part * routes : (part + 1) * routes])
    row = lax.broadcasted_iota(jnp.int32, (rows, rows), 0)
    column = lax.broadcasted_iota(jnp.int32, (rows, rows), 1)
    seen = column <= row
    for head in range(heads):
        start = 2 * width * head
        base_value = suffix_ref[:, start + width : start + 2 * width].astype(jnp.float32)
        values = (base_value + delta[:, head * width : (head + 1) * width]).astype(jnp.bfloat16)
        both = with_ones(values)
        page_both = with_ones(page_ref[:, start + width : start + 2 * width])
        for member in range(group):
            at = slice((head * group + member) * width, (head * group + member + 1) * width)
            state = attend_part(shape, query_ref, at, suffix_ref[:, start : start + width], both, None, seen)
            state = attend_part(shape, query_ref, at, page_ref[:, start : start + width], page_both, state)
            largest_ref[:, at], weighted_ref[:, at], total_ref[:, at] = state


def last_kernel(shape, read_flags, *refs):
    heads, group, width, rank, scale = shape
    places_ref, tenant_ref, blocks_ref, query_ref, largest_ref, weighted_ref, total_ref = refs[:7]
    sources, (out_ref, page_ref) = refs[7:-2], refs[-2:]
    rows = query_ref.shape[0]
    flags = read_flags(owner_of(places_ref, tenant_ref))
    copy_read(flags, page_ref, slice(0, page_ref.shape[0]), sources)
    live = lax.broadcasted_iota(jnp.int32, (rows, width), 0) < blocks_ref[0] * STRETCH
    for head in range(heads):
        start = 2 * width * head
        both = with_ones(page_ref[:, start + width : start + 2 * width])
        for member in range(group):
            at = slice((head * group + member) * width, (head * group + member + 1) * width)
            state = largest_ref[:, at], weighted_ref[:, at], total_ref[:, at]
            keys = page_ref[:, start : start + width]
            largest, weighted, total = attend_part(shape, query_ref, at, keys, both, state)
            out_ref[:, at] = jnp.where(live, weighted / total, 0.0).astype(jnp.bfloat16)


def wish_kernel(places_ref, tenant_ref, out_ref):
    other_end = jnp.where(lax.axis_index("replica") >= 2, 0, 3)
    wished = jnp.where(owner_of(places_ref, tenant_ref) == other_end, 1.0, 0.0)
    out_ref[...] = jnp.full(out_ref.shape, wished, jnp.float32)


def in_vmem(array):
    return pltpu.with_memory_space_constraint(array, pltpu.VMEM)


WHOLE = pl.BlockSpec(memory_space=pltpu.VMEM)
SCALARS = pl.BlockSpec(memory_space=pltpu.SMEM)


def cost(rows, columns, keys):
    return pl.CostEstimate(
        flops=4 * rows * columns * keys, bytes_accessed=4 * rows * columns, transcendentals=0
    )


def attend_first(shape, read_flags, scalars, inputs, parts):
    rows, columns = inputs[1].shape
    depths = [sources[0].shape[0] for sources in parts]
    cuts = [(sum(depths[:k]), sum(depths[: k + 1])) for k in range(len(depths))]
    state = pltpu.VMEM((rows, columns), jnp.float32)
    sources = [source for sources in parts for source in sources]
    return pl.pallas_call(
        functools.partial(first_kernel, shape, read_flags, cuts, len(parts[0])),
        out_shape=(pltpu.VMEM((rows, columns), jnp.bfloat16), state, state, state),
        in_specs=[SCALARS] * 3 + [WHOLE] * (5 + len(sources)),
        out_specs=(WHOLE,) * 4,
        scratch_shapes=[pltpu.VMEM((sum(depths), sources[0].shape[1]), jnp.bfloat16)],
        compiler_params=pltpu.CompilerParams(vmem_limit_bytes=VMEM_BYTES),
        cost_estimate=cost(rows, columns, sum(depths) + rows),
        name="attend_first",
    )(*scalars, *inputs, *sources)


def attend_last(shape, read_flags, scalars, states, sources):
    rows, columns = states[0].shape
    return pl.pallas_call(
        functools.partial(last_kernel, shape, read_flags),
        out_shape=jax.ShapeDtypeStruct((rows, columns), jnp.bfloat16),
        in_specs=[SCALARS] * 3 + [WHOLE] * (4 + len(sources)),
        out_specs=WHOLE,
        scratch_shapes=[pltpu.VMEM(sources[0].shape, jnp.bfloat16)],
        compiler_params=pltpu.CompilerParams(vmem_limit_bytes=VMEM_BYTES),
        cost_estimate=cost(rows, columns, sources[0].shape[0]),
        name="attend_last",
    )(*scalars, *map(in_vmem, states), *sources)


def wish(places, tenant, columns):
    return pl.pallas_call(
        wish_kernel,
        out_shape=jax.ShapeDtypeStruct((1, columns), jnp.float32),
        in_specs=[SCALARS] * 2,
        out_specs=WHOLE,
        name="wish",
    )(places, tenant)


EDGES, MIDDLE, FAR = [(0, 1), (1, 0), (2, 3), (3, 2)], [(1, 2), (2, 1)], [(1, 3), (2, 0)]
TO_INSIDE = [(3, 1), (0, 2)]
PARTS = (1, 2, 3, 2)


def moved(chunk, pairs):
    return lax.ppermute(chunk, "replica", pairs)


def line_flags(owner):
    place = lax.axis_index("replica")
    beside = jnp.where(place < 2, 1 - place, 5 - place)
    inside = (place == 1) | (place == 2)
    other = (owner != place) & (owner != beside)
    return owner == place, owner == beside, other & inside, other & jnp.logical_not(inside)


def line_attention(shape, page, places, tenant, blocks, low_of, inputs):
    count = len(PARTS)
    unit = page.shape[0] // sum(PARTS)
    page = page.reshape(page.shape[0], -1)
    own = [page[unit * sum(PARTS[:k]) : unit * sum(PARTS[: k + 1])] for k in range(count)]
    wished = wish(places, tenant, page.shape[1])
    wish_middle = moved(wished, MIDDLE)
    wish_far = moved(wished, TO_INSIDE)
    edge = [moved(own[k], EDGES) for k in range(count)]
    low = low_of()
    middle, far = [], []
    for k in range(count):
        middle.append(moved(jnp.where(wish_middle > 0, edge[k], own[k]), MIDDLE))
        far.append(moved(jnp.where(wish_far > 0, edge[k], own[k]), FAR))
    sources = list(zip(own, edge, middle, far))
    states = attend_first(
        shape, line_flags, (places, tenant, inputs[0]), (low, *inputs[1:]), sources[:-1]
    )
    return attend_last(shape, line_flags, (places, tenant, blocks), states, sources[-1])


def ring_attention(shape, page, places, tenant, blocks, low_of, inputs):
    size = lax.axis_size("replica")

    def read_flags(owner):
        place = lax.axis_index("replica")
        distance = jnp.where(owner > place, place - owner + size, place - owner)
        return [distance == offset for offset in range(READ_SPAN)]

    page = page.reshape(page.shape[0], -1)
    cut = page.shape[0] * 3 // 4
    shifts = [[(i, (i + by) % size) for i in range(size)] for by in range(1, READ_SPAN)]
    parts = [[part] + [moved(part, pairs) for pairs in shifts] for part in (page[:cut], page[cut:])]
    states = attend_first(
        shape, read_flags, (places, tenant, inputs[0]), (low_of(), *inputs[1:]), parts[:1]
    )
    return attend_last(shape, read_flags, (places, tenant, blocks), states, parts[1])


def on_device(
    suffix_hidden,
    base_query,
    suffix_key_value,
    tenant_prefix_cache,
    adapter_down,
    adapter_up_query,
    adapter_up_value,
    tenant_replica,
    tenant_of_request,
    suffix_blocks,
    request_adapter,
):
    rows = suffix_hidden.shape[0]
    heads, width = suffix_key_value.shape[1], suffix_key_value.shape[2] // 2
    group = base_query.shape[1] // (heads * width)
    adapters, rank = adapter_down.shape[0], adapter_down.shape[1] // 2
    shape = (heads, group, width, rank, math.log2(math.e) / math.sqrt(width))

    def low_of():
        down = lax.dynamic_index_in_dim(adapter_down, request_adapter[0], 0, keepdims=False)
        low = lax.dot_general(down, suffix_hidden, NT, preferred_element_type=jnp.float32)
        return swap_sum(low, "tensor")

    inputs = (
        request_adapter,
        base_query,
        adapter_up_query,
        adapter_up_value.reshape(adapters, rank, heads * width),
        suffix_key_value.reshape(rows, heads * 2 * width),
    )
    attention = line_attention if lax.axis_size("replica") == 4 else ring_attention
    return attention(
        shape, tenant_prefix_cache[0], tenant_replica, tenant_of_request, suffix_blocks,
        low_of, inputs,
    )


def solution(mesh):
    in_specs = (
        P(("group", "replica"), "tensor"),
        P(("group", "replica"), "tensor"),
        P(("group", "replica"), "tensor", None),
        P(("group", "replica"), None, "tensor", None),
        P(None, None, "tensor"),
        P(None, None, "tensor"),
        P(None, None, "tensor", None),
        P("group"),
        P(("group", "replica")),
        P(("group", "replica")),
        P(("group", "replica")),
    )
    out_specs = P(("group", "replica"), "tensor")
    return jax.shard_map(
        on_device, mesh=mesh, in_specs=in_specs, out_specs=out_specs, check_vma=False
    )
```

```python
import functools
import math

import jax
import jax.numpy as jnp
from jax import lax
from jax.experimental import pallas as pl
from jax.experimental.pallas import tpu as pltpu
from jax.sharding import PartitionSpec as P

STRETCH = 128
READ_SPAN = 4
VMEM_BYTES = 24 * 1024 * 1024
NT = (((1,), (1,)), ((), ()))
TN = (((0,), (0,)), ((), ()))


def swap_sum(value, axis):
    size = lax.axis_size(axis)
    if size & (size - 1):
        return lax.psum(value, axis)
    step = 1
    while step < size:
        value = value + lax.ppermute(value, axis, [(i, i ^ step) for i in range(size)])
        step *= 2
    return value


def head_scores(query, keys):
    return lax.dot_general(query, keys, NT, preferred_element_type=jnp.float32)


def with_ones(values):
    return jnp.concatenate([values, jnp.ones_like(values)], axis=1)


def wide(column, count):
    return jnp.concatenate([column] * count, axis=1) if count > 1 else column


def owner_of(places_ref, tenant_ref):
    return places_ref[tenant_ref[0]]


def fetch_read(flags, target, sources, semaphore):
    for flag, source in zip(flags, sources):

        @pl.when(flag)
        def _():
            pltpu.make_async_copy(source, target, semaphore).start()

    return pltpu.make_async_copy(sources[0], target, semaphore)


def attend_part(shape, query_ref, at, keys, both, state, seen=None):
    heads, group, width, rank, scale = shape
    rows, depth = query_ref.shape[0], keys.shape[0]
    scores = head_scores(query_ref[:, at], keys)
    if seen is not None:
        scores = jnp.where(seen, scores, -jnp.inf)
    largest = jnp.broadcast_to(jnp.max(scores, axis=1, keepdims=True), (rows, width))
    if state is not None:
        before, weighted_before, total_before = state
        largest = jnp.maximum(before, largest)
        fade = jnp.exp2((before - largest) * scale)
    powers = jnp.exp2((scores - wide(largest, depth // width)) * scale)
    summed = jnp.dot(powers.astype(jnp.bfloat16), both, preferred_element_type=jnp.float32)
    weighted, total = summed[:, :width], summed[:, width:]
    if state is not None:
        weighted, total = weighted + weighted_before * fade, total + total_before * fade
    return largest, weighted, total


def first_kernel(shape, read_flags, cuts, routes, *refs):
    heads, group, width, rank, scale = shape
    places_ref, tenant_ref, choice_ref, low_ref, base_ref, up_query_ref, up_value_ref, suffix_ref = refs[:8]
    sources, (query_ref, largest_ref, weighted_ref, total_ref, page_ref, semaphores) = refs[8:-6], refs[-6:]
    rows = base_ref.shape[0]
    flags = read_flags(owner_of(places_ref, tenant_ref))
    copies = [
        fetch_read(
            flags,
            page_ref.at[begin:end],
            sources[part * routes : (part + 1) * routes],
            semaphores.at[part],
        )
        for part, (begin, end) in enumerate(cuts)
    ]
    choice = choice_ref[0]
    low = low_ref[...].astype(jnp.bfloat16)
    update = lax.dot_general(low[:rank], up_query_ref[choice], TN, preferred_element_type=jnp.float32)
    query_ref[...] = (base_ref[...].astype(jnp.float32) + update).astype(jnp.bfloat16)
    delta = lax.dot_general(low[rank:], up_value_ref[choice], TN, preferred_element_type=jnp.float32)
    row = lax.broadcasted_iota(jnp.int32, (rows, rows), 0)
    column = lax.broadcasted_iota(jnp.int32, (rows, rows), 1)
    seen = column <= row
    for copy in copies:
        copy.wait()
    for head in range(heads):
        start = 2 * width * head
        base_value = suffix_ref[:, start + width : start + 2 * width].astype(jnp.float32)
        values = (base_value + delta[:, head * width : (head + 1) * width]).astype(jnp.bfloat16)
        both = with_ones(values)
        page_both = with_ones(page_ref[:, start + width : start + 2 * width])
        for member in range(group):
            at = slice((head * group + member) * width, (head * group + member + 1) * width)
            state = attend_part(shape, query_ref, at, suffix_ref[:, start : start + width], both, None, seen)
            state = attend_part(shape, query_ref, at, page_ref[:, start : start + width], page_both, state)
            largest_ref[:, at], weighted_ref[:, at], total_ref[:, at] = state


def last_kernel(shape, read_flags, *refs):
    heads, group, width, rank, scale = shape
    places_ref, tenant_ref, blocks_ref, query_ref, largest_ref, weighted_ref, total_ref = refs[:7]
    sources, (out_ref, page_ref, semaphore) = refs[7:-3], refs[-3:]
    rows = query_ref.shape[0]
    flags = read_flags(owner_of(places_ref, tenant_ref))
    fetch_read(flags, page_ref, sources, semaphore).wait()
    live = lax.broadcasted_iota(jnp.int32, (rows, width), 0) < blocks_ref[0] * STRETCH
    for head in range(heads):
        start = 2 * width * head
        both = with_ones(page_ref[:, start + width : start + 2 * width])
        for member in range(group):
            at = slice((head * group + member) * width, (head * group + member + 1) * width)
            state = largest_ref[:, at], weighted_ref[:, at], total_ref[:, at]
            keys = page_ref[:, start : start + width]
            largest, weighted, total = attend_part(shape, query_ref, at, keys, both, state)
            out_ref[:, at] = jnp.where(live, weighted / total, 0.0).astype(jnp.bfloat16)


def wish_kernel(places_ref, tenant_ref, out_ref):
    other_end = jnp.where(lax.axis_index("replica") >= 2, 0, 3)
    wished = jnp.where(owner_of(places_ref, tenant_ref) == other_end, 1.0, 0.0)
    out_ref[...] = jnp.full(out_ref.shape, wished, jnp.float32)


def in_vmem(array):
    return pltpu.with_memory_space_constraint(array, pltpu.VMEM)


def in_hbm(array):
    return pltpu.with_memory_space_constraint(array, pltpu.HBM)


def tied(values, others):
    return lax.optimization_barrier((values, others))[0]


WHOLE = pl.BlockSpec(memory_space=pltpu.VMEM)
FAR_AWAY = pl.BlockSpec(memory_space=pltpu.HBM)
SCALARS = pl.BlockSpec(memory_space=pltpu.SMEM)


def cost(rows, columns, keys):
    return pl.CostEstimate(
        flops=4 * rows * columns * keys, bytes_accessed=4 * rows * columns, transcendentals=0
    )


def attend_first(shape, read_flags, scalars, inputs, parts):
    rows, columns = inputs[1].shape
    depths = [sources[0].shape[0] for sources in parts]
    cuts = [(sum(depths[:k]), sum(depths[: k + 1])) for k in range(len(depths))]
    state = pltpu.VMEM((rows, columns), jnp.float32)
    sources = [source for sources in parts for source in sources]
    return pl.pallas_call(
        functools.partial(first_kernel, shape, read_flags, cuts, len(parts[0])),
        out_shape=(pltpu.VMEM((rows, columns), jnp.bfloat16), state, state, state),
        in_specs=[SCALARS] * 3 + [WHOLE] * 5 + [FAR_AWAY] * len(sources),
        out_specs=(WHOLE,) * 4,
        scratch_shapes=[
            pltpu.VMEM((sum(depths), sources[0].shape[1]), jnp.bfloat16),
            pltpu.SemaphoreType.DMA((len(parts),)),
        ],
        compiler_params=pltpu.CompilerParams(vmem_limit_bytes=VMEM_BYTES),
        cost_estimate=cost(rows, columns, sum(depths) + rows),
        name="attend_first",
    )(*scalars, *map(in_hbm, inputs), *map(in_hbm, sources))


def attend_last(shape, read_flags, scalars, states, sources):
    rows, columns = states[0].shape
    return pl.pallas_call(
        functools.partial(last_kernel, shape, read_flags),
        out_shape=jax.ShapeDtypeStruct((rows, columns), jnp.bfloat16),
        in_specs=[SCALARS] * 3 + [WHOLE] * 4 + [FAR_AWAY] * len(sources),
        out_specs=WHOLE,
        scratch_shapes=[pltpu.VMEM(sources[0].shape, jnp.bfloat16), pltpu.SemaphoreType.DMA],
        compiler_params=pltpu.CompilerParams(vmem_limit_bytes=VMEM_BYTES),
        cost_estimate=cost(rows, columns, sources[0].shape[0]),
        name="attend_last",
    )(*scalars, *map(in_vmem, states), *map(in_hbm, sources))


def wish(places, tenant, columns):
    return pl.pallas_call(
        wish_kernel,
        out_shape=jax.ShapeDtypeStruct((1, columns), jnp.float32),
        in_specs=[SCALARS] * 2,
        out_specs=WHOLE,
        name="wish",
    )(places, tenant)


EDGES, MIDDLE, FAR = [(0, 1), (1, 0), (2, 3), (3, 2)], [(1, 2), (2, 1)], [(1, 3), (2, 0)]
TO_INSIDE = [(3, 1), (0, 2)]
PARTS = (1, 2, 3, 2)


def moved(chunk, pairs):
    return lax.ppermute(chunk, "replica", pairs)


def line_flags(owner):
    place = lax.axis_index("replica")
    beside = jnp.where(place < 2, 1 - place, 5 - place)
    inside = (place == 1) | (place == 2)
    other = (owner != place) & (owner != beside)
    return owner == place, owner == beside, other & inside, other & jnp.logical_not(inside)


def line_attention(shape, page, places, tenant, blocks, low_of, inputs):
    count = len(PARTS)
    unit = page.shape[0] // sum(PARTS)
    own = [
        page[unit * sum(PARTS[:k]) : unit * sum(PARTS[: k + 1])].reshape(unit * PARTS[k], -1)
        for k in range(count)
    ]
    wished = wish(places, tenant, own[0].shape[1])
    wish_middle = moved(wished, MIDDLE)
    wish_far = moved(wished, TO_INSIDE)
    edge, middle, far = [moved(own[0], EDGES)], [], []
    low = low_of()
    for k in range(count):
        if k + 1 < count:
            before = (wish_middle, wish_far, edge[0]) if k == 0 else (edge[k - 1], low)
            edge.append(moved(tied(own[k + 1], before), EDGES))
        held, mine = edge[k], own[k]
        if k >= 2:
            held, mine = tied((held, mine), (middle[k - 2], far[k - 2]))
        middle.append(moved(jnp.where(wish_middle > 0, held, mine), MIDDLE))
        far.append(moved(jnp.where(wish_far > 0, held, mine), FAR))
    sources = list(zip(own, edge, middle, far))
    states = attend_first(
        shape, line_flags, (places, tenant, inputs[0]), (low, *inputs[1:]), sources[:-1]
    )
    return attend_last(shape, line_flags, (places, tenant, blocks), states, sources[-1])


def ring_attention(shape, page, places, tenant, blocks, low_of, inputs):
    size = lax.axis_size("replica")

    def read_flags(owner):
        place = lax.axis_index("replica")
        distance = jnp.where(owner > place, place - owner + size, place - owner)
        return [distance == offset for offset in range(READ_SPAN)]

    page = page.reshape(page.shape[0], -1)
    cut = page.shape[0] * 3 // 4
    shifts = [[(i, (i + by) % size) for i in range(size)] for by in range(1, READ_SPAN)]
    parts = [[part] + [moved(part, pairs) for pairs in shifts] for part in (page[:cut], page[cut:])]
    states = attend_first(
        shape, read_flags, (places, tenant, inputs[0]), (low_of(), *inputs[1:]), parts[:1]
    )
    return attend_last(shape, read_flags, (places, tenant, blocks), states, parts[1])


def on_device(
    suffix_hidden,
    base_query,
    suffix_key_value,
    tenant_prefix_cache,
    adapter_down,
    adapter_up_query,
    adapter_up_value,
    tenant_replica,
    tenant_of_request,
    suffix_blocks,
    request_adapter,
):
    rows = suffix_hidden.shape[0]
    heads, width = suffix_key_value.shape[1], suffix_key_value.shape[2] // 2
    group = base_query.shape[1] // (heads * width)
    adapters, rank = adapter_down.shape[0], adapter_down.shape[1] // 2
    shape = (heads, group, width, rank, math.log2(math.e) / math.sqrt(width))

    def low_of():
        down = lax.dynamic_index_in_dim(adapter_down, request_adapter[0], 0, keepdims=False)
        low = lax.dot_general(down, suffix_hidden, NT, preferred_element_type=jnp.float32)
        return swap_sum(low, "tensor")

    inputs = (
        request_adapter,
        base_query,
        adapter_up_query,
        adapter_up_value.reshape(adapters, rank, heads * width),
        suffix_key_value.reshape(rows, heads * 2 * width),
    )
    attention = line_attention if lax.axis_size("replica") == 4 else ring_attention
    return attention(
        shape, tenant_prefix_cache[0], tenant_replica, tenant_of_request, suffix_blocks,
        low_of, inputs,
    )


def solution(mesh):
    in_specs = (
        P(("group", "replica"), "tensor"),
        P(("group", "replica"), "tensor"),
        P(("group", "replica"), "tensor", None),
        P(("group", "replica"), None, "tensor", None),
        P(None, None, "tensor"),
        P(None, None, "tensor"),
        P(None, None, "tensor", None),
        P("group"),
        P(("group", "replica")),
        P(("group", "replica")),
        P(("group", "replica")),
    )
    out_specs = P(("group", "replica"), "tensor")
    return jax.shard_map(
        on_device, mesh=mesh, in_specs=in_specs, out_specs=out_specs, check_vma=False
    )
```

```python
import functools
import math

import jax
import jax.numpy as jnp
from jax import lax
from jax.experimental import pallas as pl
from jax.experimental.pallas import tpu as pltpu
from jax.sharding import PartitionSpec as P

STRETCH = 128
READ_SPAN = 4
VMEM_BYTES = 24 * 1024 * 1024
NT = (((1,), (1,)), ((), ()))
TN = (((0,), (0,)), ((), ()))


def swap_sum(value, axis):
    size = lax.axis_size(axis)
    if size & (size - 1):
        return lax.psum(value, axis)
    step = 1
    while step < size:
        value = value + lax.ppermute(value, axis, [(i, i ^ step) for i in range(size)])
        step *= 2
    return value


def head_scores(query, keys):
    return lax.dot_general(query, keys, NT, preferred_element_type=jnp.float32)


def with_ones(values):
    return jnp.concatenate([values, jnp.ones_like(values)], axis=1)


def wide(column, count):
    return jnp.concatenate([column] * count, axis=1) if count > 1 else column


def owner_of(places_ref, tenant_ref):
    return places_ref[tenant_ref[0]]


def fetch_read(flags, target, sources, semaphore):
    for flag, source in zip(flags, sources):

        @pl.when(flag)
        def _():
            pltpu.make_async_copy(source, target, semaphore).start()

    return pltpu.make_async_copy(sources[0], target, semaphore)


def attend_part(shape, query_ref, at, keys, both, state, seen=None):
    heads, group, width, rank, scale = shape
    rows, depth = query_ref.shape[0], keys.shape[0]
    scores = head_scores(query_ref[:, at], keys)
    if seen is not None:
        scores = jnp.where(seen, scores, -jnp.inf)
    largest = jnp.broadcast_to(jnp.max(scores, axis=1, keepdims=True), (rows, width))
    if state is not None:
        before, weighted_before, total_before = state
        largest = jnp.maximum(before, largest)
        fade = jnp.exp2((before - largest) * scale)
    powers = jnp.exp2((scores - wide(largest, depth // width)) * scale)
    summed = jnp.dot(powers.astype(jnp.bfloat16), both, preferred_element_type=jnp.float32)
    weighted, total = summed[:, :width], summed[:, width:]
    if state is not None:
        weighted, total = weighted + weighted_before * fade, total + total_before * fade
    return largest, weighted, total


def first_kernel(shape, read_flags, cuts, routes, *refs):
    heads, group, width, rank, scale = shape
    owner_ref, choice_ref, low_ref, base_ref, up_query_ref, up_value_ref, suffix_ref = refs[:7]
    sources, (query_ref, largest_ref, weighted_ref, total_ref, page_ref, semaphores) = refs[7:-6], refs[-6:]
    rows = base_ref.shape[0]
    flags = read_flags(owner_ref[0])
    copies = []
    for part, (begin, end) in enumerate(cuts):
        count = len(routes[part])
        chosen = [flags[route] for route in routes[part]]
        copies.append(
            fetch_read(chosen, page_ref.at[begin:end], sources[:count], semaphores.at[part])
        )
        sources = sources[count:]
    choice = choice_ref[0]
    low = low_ref[...].astype(jnp.bfloat16)
    update = lax.dot_general(low[:rank], up_query_ref[choice], TN, preferred_element_type=jnp.float32)
    query_ref[...] = (base_ref[...].astype(jnp.float32) + update).astype(jnp.bfloat16)
    delta = lax.dot_general(low[rank:], up_value_ref[choice], TN, preferred_element_type=jnp.float32)
    row = lax.broadcasted_iota(jnp.int32, (rows, rows), 0)
    column = lax.broadcasted_iota(jnp.int32, (rows, rows), 1)
    seen = column <= row
    for copy in copies:
        copy.wait()
    for head in range(heads):
        start = 2 * width * head
        base_value = suffix_ref[:, start + width : start + 2 * width].astype(jnp.float32)
        values = (base_value + delta[:, head * width : (head + 1) * width]).astype(jnp.bfloat16)
        both = with_ones(values)
        page_both = with_ones(page_ref[:, start + width : start + 2 * width])
        for member in range(group):
            at = slice((head * group + member) * width, (head * group + member + 1) * width)
            state = attend_part(shape, query_ref, at, suffix_ref[:, start : start + width], both, None, seen)
            state = attend_part(shape, query_ref, at, page_ref[:, start : start + width], page_both, state)
            largest_ref[:, at], weighted_ref[:, at], total_ref[:, at] = state


def last_kernel(shape, read_flags, routes, *refs):
    heads, group, width, rank, scale = shape
    owner_ref, blocks_ref, query_ref, largest_ref, weighted_ref, total_ref = refs[:6]
    sources, (out_ref, page_ref) = refs[6:-2], refs[-2:]
    rows = query_ref.shape[0]
    flags = read_flags(owner_ref[0])
    for route, source in zip(routes, sources):

        @pl.when(flags[route])
        def _():
            page_ref[...] = source[...]

    live = lax.broadcasted_iota(jnp.int32, (rows, width), 0) < blocks_ref[0] * STRETCH
    for head in range(heads):
        start = 2 * width * head
        both = with_ones(page_ref[:, start + width : start + 2 * width])
        for member in range(group):
            at = slice((head * group + member) * width, (head * group + member + 1) * width)
            state = largest_ref[:, at], weighted_ref[:, at], total_ref[:, at]
            keys = page_ref[:, start : start + width]
            largest, weighted, total = attend_part(shape, query_ref, at, keys, both, state)
            out_ref[:, at] = jnp.where(live, weighted / total, 0.0).astype(jnp.bfloat16)


def wish_kernel(places_ref, tenant_ref, after_ref, out_ref):
    other_end = jnp.where(lax.axis_index("replica") >= 2, 0, 3)
    wished = jnp.where(owner_of(places_ref, tenant_ref) == other_end, 1.0, 0.0)
    out_ref[...] = jnp.full(out_ref.shape, wished, jnp.float32)


def in_vmem(array):
    return pltpu.with_memory_space_constraint(array, pltpu.VMEM)


def in_hbm(array):
    return pltpu.with_memory_space_constraint(array, pltpu.HBM)


def tied(values, others):
    return lax.optimization_barrier((values, others))[0]


WHOLE = pl.BlockSpec(memory_space=pltpu.VMEM)
FAR_AWAY = pl.BlockSpec(memory_space=pltpu.HBM)
SCALARS = pl.BlockSpec(memory_space=pltpu.SMEM)


def cost(rows, columns, keys):
    return pl.CostEstimate(
        flops=4 * rows * columns * keys, bytes_accessed=4 * rows * columns, transcendentals=0
    )


def attend_first(shape, read_flags, scalars, inputs, parts):
    rows, columns = inputs[1].shape
    depths = [part[0][1].shape[0] for part in parts]
    cuts = [(sum(depths[:k]), sum(depths[: k + 1])) for k in range(len(depths))]
    routes = [[route for route, _ in part] for part in parts]
    sources = [source for part in parts for _, source in part]
    state = pltpu.VMEM((rows, columns), jnp.float32)
    return pl.pallas_call(
        functools.partial(first_kernel, shape, read_flags, cuts, routes),
        out_shape=(pltpu.VMEM((rows, columns), jnp.bfloat16), state, state, state),
        in_specs=[SCALARS] * 2 + [WHOLE] * 5 + [FAR_AWAY] * len(sources),
        out_specs=(WHOLE,) * 4,
        scratch_shapes=[
            pltpu.VMEM((sum(depths), sources[0].shape[1]), jnp.bfloat16),
            pltpu.SemaphoreType.DMA((len(parts),)),
        ],
        compiler_params=pltpu.CompilerParams(vmem_limit_bytes=VMEM_BYTES),
        cost_estimate=cost(rows, columns, sum(depths) + rows),
        name="attend_first",
    )(*scalars, *map(in_hbm, inputs), *map(in_hbm, sources))


def attend_last(shape, read_flags, scalars, states, part):
    rows, columns = states[0].shape
    routes, sources = zip(*part)
    return pl.pallas_call(
        functools.partial(last_kernel, shape, read_flags, routes),
        out_shape=jax.ShapeDtypeStruct((rows, columns), jnp.bfloat16),
        in_specs=[SCALARS] * 2 + [WHOLE] * (4 + len(sources)),
        out_specs=WHOLE,
        scratch_shapes=[pltpu.VMEM(sources[0].shape, jnp.bfloat16)],
        compiler_params=pltpu.CompilerParams(vmem_limit_bytes=VMEM_BYTES),
        cost_estimate=cost(rows, columns, sources[0].shape[0]),
        name="attend_last",
    )(*scalars, *map(in_vmem, states), *map(in_vmem, sources))


def wish(places, tenant, after, columns):
    return pl.pallas_call(
        wish_kernel,
        out_shape=jax.ShapeDtypeStruct((1, columns), jnp.float32),
        in_specs=[SCALARS] * 2 + [pl.BlockSpec(memory_space=pl.ANY)],
        out_specs=WHOLE,
        name="wish",
    )(places, tenant, after)


EDGES, MIDDLE, FAR = [(0, 1), (1, 0), (2, 3), (3, 2)], [(1, 2), (2, 1)], [(1, 3), (2, 0)]
TO_INSIDE = [(3, 1), (0, 2)]
PARTS = (1, 2, 3, 2)


def moved(chunk, pairs):
    return lax.ppermute(chunk, "replica", pairs)


def line_flags(owner):
    place = lax.axis_index("replica")
    beside = jnp.where(place < 2, 1 - place, 5 - place)
    inside = (place == 1) | (place == 2)
    other = (owner != place) & (owner != beside)
    return owner == place, owner == beside, other & inside, other & jnp.logical_not(inside)


def line_attention(shape, page, places, tenant, blocks, low_of, inputs):
    count = len(PARTS)
    unit = page.shape[0] // sum(PARTS)
    own = [
        page[unit * sum(PARTS[:k]) : unit * sum(PARTS[: k + 1])].reshape(unit * PARTS[k], -1)
        for k in range(count)
    ]
    edge, middle, far = [moved(own[0], EDGES)], [], []
    wished = wish(places, tenant, own[0], own[0].shape[1])
    wish_middle = moved(wished, MIDDLE)
    wish_far = moved(wished, TO_INSIDE)
    low = None
    for k in range(count):
        if k + 1 < count:
            edge.append(moved(tied(own[k + 1], (edge[k], wished) if k == 0 else edge[k]), EDGES))
        held, mine = edge[k], own[k]
        if k == 1:
            held, mine = tied((held, mine), edge[k])
        if k == 2:
            held, mine = tied((held, mine), (middle[0],))
        if k >= 3:
            held, mine = tied((held, mine), (middle[k - 2], far[k - 2], low))
        middle.append(moved(jnp.where(wish_middle > 0, held, mine), MIDDLE))
        far.append(moved(jnp.where(wish_far > 0, held, mine), FAR))
        if k == 1:
            low = low_of((middle[0], far[0], edge[1]))
    parts = [list(enumerate(routes)) for routes in zip(own, edge, middle, far)]
    owner = lax.dynamic_slice(places, tied(tenant, edge[1]), (1,))
    states = attend_first(
        shape, line_flags, (owner, inputs[0]), (low, *inputs[1:]), parts[:-1]
    )
    return attend_last(shape, line_flags, (owner, blocks), states, parts[-1])


def ring_attention(shape, page, places, tenant, blocks, low_of, inputs):
    size = lax.axis_size("replica")

    def read_flags(owner):
        place = lax.axis_index("replica")
        distance = jnp.where(owner > place, place - owner + size, place - owner)
        return [distance == offset for offset in range(READ_SPAN)]

    page = page.reshape(page.shape[0], -1)
    cut = page.shape[0] * 3 // 4
    shifts = [[(i, (i + by) % size) for i in range(size)] for by in range(1, READ_SPAN)]
    parts = [
        list(enumerate([part] + [moved(part, pairs) for pairs in shifts]))
        for part in (page[:cut], page[cut:])
    ]
    owner = lax.dynamic_slice(places, tenant, (1,))
    states = attend_first(
        shape, read_flags, (owner, inputs[0]), (low_of(page), *inputs[1:]), parts[:1]
    )
    return attend_last(shape, read_flags, (owner, blocks), states, parts[1])


def on_device(
    suffix_hidden,
    base_query,
    suffix_key_value,
    tenant_prefix_cache,
    adapter_down,
    adapter_up_query,
    adapter_up_value,
    tenant_replica,
    tenant_of_request,
    suffix_blocks,
    request_adapter,
):
    rows = suffix_hidden.shape[0]
    heads, width = suffix_key_value.shape[1], suffix_key_value.shape[2] // 2
    group = base_query.shape[1] // (heads * width)
    adapters, rank = adapter_down.shape[0], adapter_down.shape[1] // 2
    shape = (heads, group, width, rank, math.log2(math.e) / math.sqrt(width))

    def low_of(before):
        hidden = tied(suffix_hidden, before)
        down = lax.dynamic_index_in_dim(adapter_down, request_adapter[0], 0, keepdims=False)
        low = lax.dot_general(down, hidden, NT, preferred_element_type=jnp.float32)
        return swap_sum(low, "tensor")

    inputs = (
        request_adapter,
        base_query,
        adapter_up_query,
        adapter_up_value.reshape(adapters, rank, heads * width),
        suffix_key_value.reshape(rows, heads * 2 * width),
    )
    attention = line_attention if lax.axis_size("replica") == 4 else ring_attention
    return attention(
        shape, tenant_prefix_cache[0], tenant_replica, tenant_of_request, suffix_blocks,
        low_of, inputs,
    )


def solution(mesh):
    in_specs = (
        P(("group", "replica"), "tensor"),
        P(("group", "replica"), "tensor"),
        P(("group", "replica"), "tensor", None),
        P(("group", "replica"), None, "tensor", None),
        P(None, None, "tensor"),
        P(None, None, "tensor"),
        P(None, None, "tensor", None),
        P("group"),
        P(("group", "replica")),
        P(("group", "replica")),
        P(("group", "replica")),
    )
    out_specs = P(("group", "replica"), "tensor")
    return jax.shard_map(
        on_device, mesh=mesh, in_specs=in_specs, out_specs=out_specs, check_vma=False
    )
```

```python
import functools
import math

import jax
import jax.numpy as jnp
from jax import lax
from jax.experimental import pallas as pl
from jax.experimental.pallas import tpu as pltpu
from jax.sharding import PartitionSpec as P

STRETCH = 128
READ_SPAN = 4
VMEM_BYTES = 24 * 1024 * 1024
NT = (((1,), (1,)), ((), ()))
TN = (((0,), (0,)), ((), ()))


def swap_sum(value, axis):
    size = lax.axis_size(axis)
    if size & (size - 1):
        return lax.psum(value, axis)
    step = 1
    while step < size:
        value = value + lax.ppermute(value, axis, [(i, i ^ step) for i in range(size)])
        step *= 2
    return value


def head_scores(query, keys):
    return lax.dot_general(query, keys, NT, preferred_element_type=jnp.float32)


def with_ones(values):
    return jnp.concatenate([values, jnp.ones_like(values)], axis=1)


def wide(column, count):
    return jnp.concatenate([column] * count, axis=1) if count > 1 else column


def owner_of(places_ref, tenant_ref):
    return places_ref[tenant_ref[0]]


def fetch_read(flags, target, sources, semaphore):
    for flag, source in zip(flags, sources):

        @pl.when(flag)
        def _():
            pltpu.make_async_copy(source, target, semaphore).start()

    return pltpu.make_async_copy(sources[0], target, semaphore)


def attend_part(shape, query_ref, at, keys, both, state, seen=None):
    heads, group, width, rank, scale = shape
    rows, depth = query_ref.shape[0], keys.shape[0]
    scores = head_scores(query_ref[:, at], keys)
    if seen is not None:
        scores = jnp.where(seen, scores, -jnp.inf)
    largest = jnp.broadcast_to(jnp.max(scores, axis=1, keepdims=True), (rows, width))
    if state is not None:
        before, weighted_before, total_before = state
        largest = jnp.maximum(before, largest)
        fade = jnp.exp2((before - largest) * scale)
    powers = jnp.exp2((scores - wide(largest, depth // width)) * scale)
    summed = jnp.dot(powers.astype(jnp.bfloat16), both, preferred_element_type=jnp.float32)
    weighted, total = summed[:, :width], summed[:, width:]
    if state is not None:
        weighted, total = weighted + weighted_before * fade, total + total_before * fade
    return largest, weighted, total


def first_kernel(shape, read_flags, cuts, routes, *refs):
    heads, group, width, rank, scale = shape
    owner_ref, choice_ref, low_ref, base_ref, up_query_ref, up_value_ref, suffix_ref = refs[:7]
    sources, (query_ref, largest_ref, weighted_ref, total_ref, page_ref, semaphores) = refs[7:-6], refs[-6:]
    rows = base_ref.shape[0]
    flags = read_flags(owner_ref[0])
    copies = []
    for part, (begin, end) in enumerate(cuts):
        count = len(routes[part])
        chosen = [flags[route] for route in routes[part]]
        copies.append(
            fetch_read(chosen, page_ref.at[begin:end], sources[:count], semaphores.at[part])
        )
        sources = sources[count:]
    choice = choice_ref[0]
    low = low_ref[...].astype(jnp.bfloat16)
    update = lax.dot_general(low[:rank], up_query_ref[choice], TN, preferred_element_type=jnp.float32)
    query_ref[...] = (base_ref[...].astype(jnp.float32) + update).astype(jnp.bfloat16)
    delta = lax.dot_general(low[rank:], up_value_ref[choice], TN, preferred_element_type=jnp.float32)
    row = lax.broadcasted_iota(jnp.int32, (rows, rows), 0)
    column = lax.broadcasted_iota(jnp.int32, (rows, rows), 1)
    seen = column <= row
    for copy in copies:
        copy.wait()
    for head in range(heads):
        start = 2 * width * head
        base_value = suffix_ref[:, start + width : start + 2 * width].astype(jnp.float32)
        values = (base_value + delta[:, head * width : (head + 1) * width]).astype(jnp.bfloat16)
        both = with_ones(values)
        page_both = with_ones(page_ref[:, start + width : start + 2 * width])
        for member in range(group):
            at = slice((head * group + member) * width, (head * group + member + 1) * width)
            state = attend_part(shape, query_ref, at, suffix_ref[:, start : start + width], both, None, seen)
            state = attend_part(shape, query_ref, at, page_ref[:, start : start + width], page_both, state)
            largest_ref[:, at], weighted_ref[:, at], total_ref[:, at] = state


def last_kernel(shape, read_flags, routes, *refs):
    heads, group, width, rank, scale = shape
    owner_ref, blocks_ref, query_ref, largest_ref, weighted_ref, total_ref = refs[:6]
    sources, (out_ref, page_ref) = refs[6:-2], refs[-2:]
    rows = query_ref.shape[0]
    flags = read_flags(owner_ref[0])
    for route, source in zip(routes, sources):

        @pl.when(flags[route])
        def _():
            page_ref[...] = source[...]

    live = lax.broadcasted_iota(jnp.int32, (rows, width), 0) < blocks_ref[0] * STRETCH
    for head in range(heads):
        start = 2 * width * head
        both = with_ones(page_ref[:, start + width : start + 2 * width])
        for member in range(group):
            at = slice((head * group + member) * width, (head * group + member + 1) * width)
            state = largest_ref[:, at], weighted_ref[:, at], total_ref[:, at]
            keys = page_ref[:, start : start + width]
            largest, weighted, total = attend_part(shape, query_ref, at, keys, both, state)
            out_ref[:, at] = jnp.where(live, weighted / total, 0.0).astype(jnp.bfloat16)


def wish_kernel(places_ref, tenant_ref, after_ref, out_ref):
    other_end = jnp.where(lax.axis_index("replica") >= 2, 0, 3)
    wished = jnp.where(owner_of(places_ref, tenant_ref) == other_end, 1.0, 0.0)
    out_ref[...] = jnp.full(out_ref.shape, wished, jnp.float32)


def in_vmem(array):
    return pltpu.with_memory_space_constraint(array, pltpu.VMEM)


def in_hbm(array):
    return pltpu.with_memory_space_constraint(array, pltpu.HBM)


def tied(values, others):
    return lax.optimization_barrier((values, others))[0]


WHOLE = pl.BlockSpec(memory_space=pltpu.VMEM)
FAR_AWAY = pl.BlockSpec(memory_space=pltpu.HBM)
SCALARS = pl.BlockSpec(memory_space=pltpu.SMEM)


def cost(rows, columns, keys):
    return pl.CostEstimate(
        flops=4 * rows * columns * keys, bytes_accessed=4 * rows * columns, transcendentals=0
    )


def attend_first(shape, read_flags, scalars, inputs, parts):
    rows, columns = inputs[1].shape
    depths = [part[0][1].shape[0] for part in parts]
    cuts = [(sum(depths[:k]), sum(depths[: k + 1])) for k in range(len(depths))]
    routes = [[route for route, _ in part] for part in parts]
    sources = [source for part in parts for _, source in part]
    state = pltpu.VMEM((rows, columns), jnp.float32)
    return pl.pallas_call(
        functools.partial(first_kernel, shape, read_flags, cuts, routes),
        out_shape=(pltpu.VMEM((rows, columns), jnp.bfloat16), state, state, state),
        in_specs=[SCALARS] * 2 + [WHOLE] * 5 + [FAR_AWAY] * len(sources),
        out_specs=(WHOLE,) * 4,
        scratch_shapes=[
            pltpu.VMEM((sum(depths), sources[0].shape[1]), jnp.bfloat16),
            pltpu.SemaphoreType.DMA((len(parts),)),
        ],
        compiler_params=pltpu.CompilerParams(vmem_limit_bytes=VMEM_BYTES),
        cost_estimate=cost(rows, columns, sum(depths) + rows),
        name="attend_first",
    )(*scalars, *map(in_hbm, inputs), *map(in_hbm, sources))


def attend_last(shape, read_flags, scalars, states, part):
    rows, columns = states[0].shape
    routes, sources = zip(*part)
    return pl.pallas_call(
        functools.partial(last_kernel, shape, read_flags, routes),
        out_shape=jax.ShapeDtypeStruct((rows, columns), jnp.bfloat16),
        in_specs=[SCALARS] * 2 + [WHOLE] * (4 + len(sources)),
        out_specs=WHOLE,
        scratch_shapes=[pltpu.VMEM(sources[0].shape, jnp.bfloat16)],
        compiler_params=pltpu.CompilerParams(vmem_limit_bytes=VMEM_BYTES),
        cost_estimate=cost(rows, columns, sources[0].shape[0]),
        name="attend_last",
    )(*scalars, *map(in_vmem, states), *map(in_vmem, sources))


def wish(places, tenant, after, columns):
    return pl.pallas_call(
        wish_kernel,
        out_shape=jax.ShapeDtypeStruct((1, columns), jnp.float32),
        in_specs=[SCALARS] * 2 + [pl.BlockSpec(memory_space=pl.ANY)],
        out_specs=WHOLE,
        name="wish",
    )(places, tenant, after)


EDGES, MIDDLE, FAR = [(0, 1), (1, 0), (2, 3), (3, 2)], [(1, 2), (2, 1)], [(1, 3), (2, 0)]
TO_INSIDE = [(3, 1), (0, 2)]
PARTS = (1, 3, 4)


def moved(chunk, pairs):
    return lax.ppermute(chunk, "replica", pairs)


def line_flags(owner):
    place = lax.axis_index("replica")
    beside = jnp.where(place < 2, 1 - place, 5 - place)
    inside = (place == 1) | (place == 2)
    other = (owner != place) & (owner != beside)
    return owner == place, owner == beside, other & inside, other & jnp.logical_not(inside)


def line_attention(shape, page, places, tenant, blocks, low_of, inputs):
    count = len(PARTS)
    unit = page.shape[0] // sum(PARTS)
    own = [
        page[unit * sum(PARTS[:k]) : unit * sum(PARTS[: k + 1])].reshape(unit * PARTS[k], -1)
        for k in range(count)
    ]
    edge, middle, far = [moved(own[0], EDGES)], [], []
    wished = wish(places, tenant, own[0], own[0].shape[1])
    wish_middle = moved(wished, MIDDLE)
    wish_far = moved(wished, TO_INSIDE)
    low = None
    for k in range(count):
        if k == 0:
            edge.append(moved(tied(own[1], (edge[0], (wish_middle, wish_far))), EDGES))
        held, mine = edge[k], own[k]
        if k == 1:
            held, mine = tied((held, mine), (middle[0], far[0]))
        if k == 2:
            held, mine = tied((held, mine), (middle[0], far[0]))
        if k >= 3:
            held, mine = tied((held, mine), (middle[k - 2], far[k - 2], low))
        inner, outer = jnp.where(wish_middle > 0, held, mine), jnp.where(wish_far > 0, held, mine)
        if 1 <= k < count - 1:
            edge.append(moved(tied(own[k + 1], (inner, outer)), EDGES))
        middle.append(moved(inner, MIDDLE))
        far.append(moved(outer, FAR))
        if k == 1:
            low = low_of(middle[1])
    parts = [list(enumerate(routes)) for routes in zip(own, edge, middle, far)]
    owner = lax.dynamic_slice(places, tied(tenant, edge[1]), (1,))
    states = attend_first(
        shape, line_flags, (owner, inputs[0]), (low, *inputs[1:]), parts[:-1]
    )
    return attend_last(shape, line_flags, (owner, blocks), states, parts[-1])


def ring_attention(shape, page, places, tenant, blocks, low_of, inputs):
    size = lax.axis_size("replica")

    def read_flags(owner):
        place = lax.axis_index("replica")
        distance = jnp.where(owner > place, place - owner + size, place - owner)
        return [distance == offset for offset in range(READ_SPAN)]

    page = page.reshape(page.shape[0], -1)
    cut = page.shape[0] * 3 // 4
    shifts = [[(i, (i + by) % size) for i in range(size)] for by in range(1, READ_SPAN)]
    parts = [
        list(enumerate([part] + [moved(part, pairs) for pairs in shifts]))
        for part in (page[:cut], page[cut:])
    ]
    owner = lax.dynamic_slice(places, tenant, (1,))
    states = attend_first(
        shape, read_flags, (owner, inputs[0]), (low_of(page), *inputs[1:]), parts[:1]
    )
    return attend_last(shape, read_flags, (owner, blocks), states, parts[1])


def on_device(
    suffix_hidden,
    base_query,
    suffix_key_value,
    tenant_prefix_cache,
    adapter_down,
    adapter_up_query,
    adapter_up_value,
    tenant_replica,
    tenant_of_request,
    suffix_blocks,
    request_adapter,
):
    rows = suffix_hidden.shape[0]
    heads, width = suffix_key_value.shape[1], suffix_key_value.shape[2] // 2
    group = base_query.shape[1] // (heads * width)
    adapters, rank = adapter_down.shape[0], adapter_down.shape[1] // 2
    shape = (heads, group, width, rank, math.log2(math.e) / math.sqrt(width))

    def low_of(before):
        hidden = tied(suffix_hidden, before)
        down = lax.dynamic_index_in_dim(adapter_down, request_adapter[0], 0, keepdims=False)
        low = lax.dot_general(down, hidden, NT, preferred_element_type=jnp.float32)
        return swap_sum(low, "tensor")

    inputs = (
        request_adapter,
        base_query,
        adapter_up_query,
        adapter_up_value.reshape(adapters, rank, heads * width),
        suffix_key_value.reshape(rows, heads * 2 * width),
    )
    attention = line_attention if lax.axis_size("replica") == 4 else ring_attention
    return attention(
        shape, tenant_prefix_cache[0], tenant_replica, tenant_of_request, suffix_blocks,
        low_of, inputs,
    )


def solution(mesh):
    in_specs = (
        P(("group", "replica"), "tensor"),
        P(("group", "replica"), "tensor"),
        P(("group", "replica"), "tensor", None),
        P(("group", "replica"), None, "tensor", None),
        P(None, None, "tensor"),
        P(None, None, "tensor"),
        P(None, None, "tensor", None),
        P("group"),
        P(("group", "replica")),
        P(("group", "replica")),
        P(("group", "replica")),
    )
    out_specs = P(("group", "replica"), "tensor")
    return jax.shard_map(
        on_device, mesh=mesh, in_specs=in_specs, out_specs=out_specs, check_vma=False
    )
```

```python
import functools
import math

import jax
import jax.numpy as jnp
from jax import lax
from jax.experimental import pallas as pl
from jax.experimental.pallas import tpu as pltpu
from jax.sharding import PartitionSpec as P

STRETCH = 128
READ_SPAN = 4
VMEM_BYTES = 24 * 1024 * 1024
NT = (((1,), (1,)), ((), ()))
TN = (((0,), (0,)), ((), ()))


def swap_sum(value, axis):
    size = lax.axis_size(axis)
    if size & (size - 1):
        return lax.psum(value, axis)
    step = 1
    while step < size:
        value = value + lax.ppermute(value, axis, [(i, i ^ step) for i in range(size)])
        step *= 2
    return value


def head_scores(query, keys):
    return lax.dot_general(query, keys, NT, preferred_element_type=jnp.float32)


def with_ones(values):
    return jnp.concatenate([values, jnp.ones_like(values)], axis=1)


def wide(column, count):
    return jnp.concatenate([column] * count, axis=1) if count > 1 else column


def owner_of(places_ref, tenant_ref):
    return places_ref[tenant_ref[0]]


def fetch_read(flags, target, sources, semaphore):
    for flag, source in zip(flags, sources):

        @pl.when(flag)
        def _():
            pltpu.make_async_copy(source, target, semaphore).start()

    return pltpu.make_async_copy(sources[0], target, semaphore)


def attend_part(shape, query_ref, at, keys, both, state, seen=None):
    heads, group, width, rank, scale = shape
    rows, depth = query_ref.shape[0], keys.shape[0]
    scores = head_scores(query_ref[:, at], keys)
    if seen is not None:
        scores = jnp.where(seen, scores, -jnp.inf)
    largest = jnp.broadcast_to(jnp.max(scores, axis=1, keepdims=True), (rows, width))
    if state is not None:
        before, weighted_before, total_before = state
        largest = jnp.maximum(before, largest)
        fade = jnp.exp2((before - largest) * scale)
    powers = jnp.exp2((scores - wide(largest, depth // width)) * scale)
    summed = jnp.dot(powers.astype(jnp.bfloat16), both, preferred_element_type=jnp.float32)
    weighted, total = summed[:, :width], summed[:, width:]
    if state is not None:
        weighted, total = weighted + weighted_before * fade, total + total_before * fade
    return largest, weighted, total


def first_kernel(shape, read_flags, cuts, routes, *refs):
    heads, group, width, rank, scale = shape
    owner_ref, choice_ref, low_ref, base_ref, up_query_ref, up_value_ref, suffix_ref = refs[:7]
    sources, (query_ref, largest_ref, weighted_ref, total_ref, page_ref, semaphores) = refs[7:-6], refs[-6:]
    rows = base_ref.shape[0]
    flags = read_flags(owner_ref[0])
    copies = []
    for part, (begin, end) in enumerate(cuts):
        count = len(routes[part])
        chosen = [flags[route] for route in routes[part]]
        copies.append(
            fetch_read(chosen, page_ref.at[begin:end], sources[:count], semaphores.at[part])
        )
        sources = sources[count:]
    choice = choice_ref[0]
    low = low_ref[...].astype(jnp.bfloat16)
    update = lax.dot_general(low[:rank], up_query_ref[choice], TN, preferred_element_type=jnp.float32)
    query_ref[...] = (base_ref[...].astype(jnp.float32) + update).astype(jnp.bfloat16)
    delta = lax.dot_general(low[rank:], up_value_ref[choice], TN, preferred_element_type=jnp.float32)
    row = lax.broadcasted_iota(jnp.int32, (rows, rows), 0)
    column = lax.broadcasted_iota(jnp.int32, (rows, rows), 1)
    seen = column <= row
    for copy in copies:
        copy.wait()
    for head in range(heads):
        start = 2 * width * head
        base_value = suffix_ref[:, start + width : start + 2 * width].astype(jnp.float32)
        values = (base_value + delta[:, head * width : (head + 1) * width]).astype(jnp.bfloat16)
        both = with_ones(values)
        page_both = with_ones(page_ref[:, start + width : start + 2 * width])
        for member in range(group):
            at = slice((head * group + member) * width, (head * group + member + 1) * width)
            state = attend_part(shape, query_ref, at, suffix_ref[:, start : start + width], both, None, seen)
            state = attend_part(shape, query_ref, at, page_ref[:, start : start + width], page_both, state)
            largest_ref[:, at], weighted_ref[:, at], total_ref[:, at] = state


def last_kernel(shape, read_flags, routes, *refs):
    heads, group, width, rank, scale = shape
    owner_ref, blocks_ref, query_ref, largest_ref, weighted_ref, total_ref = refs[:6]
    sources, (out_ref, page_ref) = refs[6:-2], refs[-2:]
    rows = query_ref.shape[0]
    flags = read_flags(owner_ref[0])
    for route, source in zip(routes, sources):

        @pl.when(flags[route])
        def _():
            page_ref[...] = source[...]

    live = lax.broadcasted_iota(jnp.int32, (rows, width), 0) < blocks_ref[0] * STRETCH
    for head in range(heads):
        start = 2 * width * head
        both = with_ones(page_ref[:, start + width : start + 2 * width])
        for member in range(group):
            at = slice((head * group + member) * width, (head * group + member + 1) * width)
            state = largest_ref[:, at], weighted_ref[:, at], total_ref[:, at]
            keys = page_ref[:, start : start + width]
            largest, weighted, total = attend_part(shape, query_ref, at, keys, both, state)
            out_ref[:, at] = jnp.where(live, weighted / total, 0.0).astype(jnp.bfloat16)


def wish_kernel(places_ref, tenant_ref, after_ref, out_ref):
    other_end = jnp.where(lax.axis_index("replica") >= 2, 0, 3)
    wished = jnp.where(owner_of(places_ref, tenant_ref) == other_end, 1.0, 0.0)
    out_ref[...] = jnp.full(out_ref.shape, wished, jnp.float32)


def in_vmem(array):
    return pltpu.with_memory_space_constraint(array, pltpu.VMEM)


def in_hbm(array):
    return pltpu.with_memory_space_constraint(array, pltpu.HBM)


def tied(values, others):
    return lax.optimization_barrier((values, others))[0]


WHOLE = pl.BlockSpec(memory_space=pltpu.VMEM)
FAR_AWAY = pl.BlockSpec(memory_space=pltpu.HBM)
SCALARS = pl.BlockSpec(memory_space=pltpu.SMEM)


def cost(rows, columns, keys):
    return pl.CostEstimate(
        flops=4 * rows * columns * keys, bytes_accessed=4 * rows * columns, transcendentals=0
    )


def attend_first(shape, read_flags, scalars, inputs, parts):
    rows, columns = inputs[1].shape
    depths = [part[0][1].shape[0] for part in parts]
    cuts = [(sum(depths[:k]), sum(depths[: k + 1])) for k in range(len(depths))]
    routes = [[route for route, _ in part] for part in parts]
    sources = [source for part in parts for _, source in part]
    state = pltpu.VMEM((rows, columns), jnp.float32)
    return pl.pallas_call(
        functools.partial(first_kernel, shape, read_flags, cuts, routes),
        out_shape=(pltpu.VMEM((rows, columns), jnp.bfloat16), state, state, state),
        in_specs=[SCALARS] * 2 + [WHOLE] * 5 + [FAR_AWAY] * len(sources),
        out_specs=(WHOLE,) * 4,
        scratch_shapes=[
            pltpu.VMEM((sum(depths), sources[0].shape[1]), jnp.bfloat16),
            pltpu.SemaphoreType.DMA((len(parts),)),
        ],
        compiler_params=pltpu.CompilerParams(vmem_limit_bytes=VMEM_BYTES),
        cost_estimate=cost(rows, columns, sum(depths) + rows),
        name="attend_first",
    )(*scalars, *map(in_hbm, inputs), *map(in_hbm, sources))


def attend_last(shape, read_flags, scalars, states, part):
    rows, columns = states[0].shape
    routes, sources = zip(*part)
    return pl.pallas_call(
        functools.partial(last_kernel, shape, read_flags, routes),
        out_shape=jax.ShapeDtypeStruct((rows, columns), jnp.bfloat16),
        in_specs=[SCALARS] * 2 + [WHOLE] * (4 + len(sources)),
        out_specs=WHOLE,
        scratch_shapes=[pltpu.VMEM(sources[0].shape, jnp.bfloat16)],
        compiler_params=pltpu.CompilerParams(vmem_limit_bytes=VMEM_BYTES),
        cost_estimate=cost(rows, columns, sources[0].shape[0]),
        name="attend_last",
    )(*scalars, *map(in_vmem, states), *map(in_vmem, sources))


def wish(places, tenant, after, columns):
    return pl.pallas_call(
        wish_kernel,
        out_shape=jax.ShapeDtypeStruct((1, columns), jnp.float32),
        in_specs=[SCALARS] * 2 + [pl.BlockSpec(memory_space=pl.ANY)],
        out_specs=WHOLE,
        name="wish",
    )(places, tenant, after)


EDGES, MIDDLE, FAR = [(0, 1), (1, 0), (2, 3), (3, 2)], [(1, 2), (2, 1)], [(1, 3), (2, 0)]
TO_INSIDE = [(3, 1), (0, 2)]
PARTS = (3, 7, 6)


def moved(chunk, pairs):
    return lax.ppermute(chunk, "replica", pairs)


def line_flags(owner):
    place = lax.axis_index("replica")
    beside = jnp.where(place < 2, 1 - place, 5 - place)
    inside = (place == 1) | (place == 2)
    other = (owner != place) & (owner != beside)
    return owner == place, owner == beside, other & inside, other & jnp.logical_not(inside)


def line_attention(shape, page, places, tenant, blocks, low_of, inputs):
    count = len(PARTS)
    unit = page.shape[0] // sum(PARTS)
    own = [
        page[unit * sum(PARTS[:k]) : unit * sum(PARTS[: k + 1])].reshape(unit * PARTS[k], -1)
        for k in range(count)
    ]
    edge, middle, far = [moved(own[0], EDGES)], [], []
    wished = wish(places, tenant, own[0], own[0].shape[1])
    wish_middle = moved(wished, MIDDLE)
    wish_far = moved(wished, TO_INSIDE)
    low = None
    for k in range(count):
        if k == 0:
            edge.append(moved(tied(own[1], (edge[0], (wish_middle, wish_far))), EDGES))
        held, mine = edge[k], own[k]
        if k == 1:
            held, mine = tied((held, mine), (middle[0], far[0]))
        if k == 2:
            held, mine = tied((held, mine), (middle[0], far[0]))
        if k >= 3:
            held, mine = tied((held, mine), (middle[k - 2], far[k - 2], low))
        inner, outer = jnp.where(wish_middle > 0, held, mine), jnp.where(wish_far > 0, held, mine)
        if 1 <= k < count - 1:
            edge.append(moved(tied(own[k + 1], (inner, outer)), EDGES))
        middle.append(moved(inner, MIDDLE))
        far.append(moved(outer, FAR))
        if k == 1:
            low = low_of(middle[1])
    parts = [list(enumerate(routes)) for routes in zip(own, edge, middle, far)]
    owner = lax.dynamic_slice(places, tied(tenant, edge[1]), (1,))
    states = attend_first(
        shape, line_flags, (owner, inputs[0]), (low, *inputs[1:]), parts[:-1]
    )
    return attend_last(shape, line_flags, (owner, blocks), states, parts[-1])


def ring_attention(shape, page, places, tenant, blocks, low_of, inputs):
    size = lax.axis_size("replica")

    def read_flags(owner):
        place = lax.axis_index("replica")
        distance = jnp.where(owner > place, place - owner + size, place - owner)
        return [distance == offset for offset in range(READ_SPAN)]

    page = page.reshape(page.shape[0], -1)
    cut = page.shape[0] * 3 // 4
    shifts = [[(i, (i + by) % size) for i in range(size)] for by in range(1, READ_SPAN)]
    parts = [
        list(enumerate([part] + [moved(part, pairs) for pairs in shifts]))
        for part in (page[:cut], page[cut:])
    ]
    owner = lax.dynamic_slice(places, tenant, (1,))
    states = attend_first(
        shape, read_flags, (owner, inputs[0]), (low_of(page), *inputs[1:]), parts[:1]
    )
    return attend_last(shape, read_flags, (owner, blocks), states, parts[1])


def on_device(
    suffix_hidden,
    base_query,
    suffix_key_value,
    tenant_prefix_cache,
    adapter_down,
    adapter_up_query,
    adapter_up_value,
    tenant_replica,
    tenant_of_request,
    suffix_blocks,
    request_adapter,
):
    rows = suffix_hidden.shape[0]
    heads, width = suffix_key_value.shape[1], suffix_key_value.shape[2] // 2
    group = base_query.shape[1] // (heads * width)
    adapters, rank = adapter_down.shape[0], adapter_down.shape[1] // 2
    shape = (heads, group, width, rank, math.log2(math.e) / math.sqrt(width))

    def low_of(before):
        hidden = tied(suffix_hidden, before)
        down = lax.dynamic_index_in_dim(adapter_down, request_adapter[0], 0, keepdims=False)
        low = lax.dot_general(down, hidden, NT, preferred_element_type=jnp.float32)
        return swap_sum(low, "tensor")

    inputs = (
        request_adapter,
        base_query,
        adapter_up_query,
        adapter_up_value.reshape(adapters, rank, heads * width),
        suffix_key_value.reshape(rows, heads * 2 * width),
    )
    attention = line_attention if lax.axis_size("replica") == 4 else ring_attention
    return attention(
        shape, tenant_prefix_cache[0], tenant_replica, tenant_of_request, suffix_blocks,
        low_of, inputs,
    )


def solution(mesh):
    in_specs = (
        P(("group", "replica"), "tensor"),
        P(("group", "replica"), "tensor"),
        P(("group", "replica"), "tensor", None),
        P(("group", "replica"), None, "tensor", None),
        P(None, None, "tensor"),
        P(None, None, "tensor"),
        P(None, None, "tensor", None),
        P("group"),
        P(("group", "replica")),
        P(("group", "replica")),
        P(("group", "replica")),
    )
    out_specs = P(("group", "replica"), "tensor")
    return jax.shard_map(
        on_device, mesh=mesh, in_specs=in_specs, out_specs=out_specs, check_vma=False
    )
```
